32 devices in a mesh: groups: 2 (over y), expert: 16 (over z, x, core).
Axes of the slice: x: 2, y: 2, z: 4, core: 2. Of those that a mesh axis runs over, the one named last changes fastest.
Arguments:
- attn_heads: bfloat16 [4096, 4096], P(('groups', 'expert')), parts along dimension 0, may hold values from -6 to 6
- residual: bfloat16 [4096, 2048], P(('groups', 'expert')), parts along dimension 0, may hold values from -6 to 6
- w_out: bfloat16 [4096, 2048], P('expert'), may hold values from -0.09375 to 0.09375
- norm_gain: float32 [2048], replicated, may hold values from 0.1 to 1.9
- expert_ids: int32 [4096, 8], P(('groups', 'expert')), parts along dimension 0, may hold values from 0 to 15, all different within a row; in each aligned block of 128 rows (0 to 127, 128 to 255, ...) at most 80 rows name the same one
- route_num: int32 [4096, 8], P(('groups', 'expert')), parts along dimension 0, may hold values from 1 to 16
- w_gate: bfloat16 [16, 2048, 768], P('expert'), may hold values from -0.125 to 0.125
- w_up: bfloat16 [16, 2048, 768], P('expert'), may hold values from -0.125 to 0.125
- w_down: bfloat16 [16, 768, 2048], P('expert'), may hold values from -0.21875 to 0.21875
Outputs:
- mid_state: bfloat16 [4096, 2048], P(('groups', 'expert')), parts along dimension 0
- expert_out: bfloat16 [4096, 2048], P(('groups', 'expert')), parts along dimension 0
The draws below stay inside these ranges and needn't reach their ends.
There are 2 independent parts, one for each index of `groups`. The reference program is written for one: setup_inputs(seed, part) draws one part's arguments, and reference() takes and returns one part's arrays. A program takes and returns all parts, laid end to end along the dimension named above; an argument that names none is the same for every part. Nothing has to cross between parts.
Inputs may be any that keep to these rules, and one draw needn't show every extreme that they name: `expert_ids`: each token names 8 different experts; among the 128 tokens of one device no expert is named more than 80 times, a bound that some block reaches.
All inputs are finite; a program needn't handle non-finite values.
Results may differ from the reference program's by a relative error of at most 0.0095.
Values may be sent and summed in bfloat16 or wider, within the bound.
A program may use at most 128 MiB of HBM per device.

```python
import math
import jax
import jax.numpy as jnp
import numpy as np
from jax import lax

D = 2048
FFE = 768
TOPK = 8
TOK_DEV = 128
ATT = 4096
TOKENS = 2048
EXPERTS = 16
CAP = 80
N_EXPERT = 16


def plant(entries, own_key, smallest, high):
    longest = entries.shape.index(max(entries.shape))
    spots = []
    for shift in (0, 1):
        where = [jax.random.randint(jax.random.fold_in(own_key, axis), (), 0, length) for axis, length in enumerate(entries.shape)]
        where[longest] = (where[longest] + shift) % entries.shape[longest]
        spots.append(tuple(where))
    return entries.at[spots[0]].set(smallest).at[spots[1]].set(high)


def block_levels(stream_key, dims, cuts, smallest, top_value):
    loudness, own = 1.0, jax.random.fold_in(stream_key, 6)
    for axis_at, shards_of in cuts:
        steps = jnp.exp(jax.random.uniform(jax.random.fold_in(own, axis_at), (shards_of,), jnp.float32, smallest / len(cuts), top_value / len(cuts)))
        loudness = loudness * jnp.repeat(steps, dims[axis_at] // shards_of).reshape([-1 if axis == axis_at else 1 for axis in range(len(dims))])
    return loudness


def routed_block(stream_key, own, number, rows, number_of, top, bound, slope):
    order = jax.random.permutation(stream_key, number_of)
    packed, ordinary = shares(number_of, rows * top, bound, slope, True), shares(number_of, rows * top, bound, slope, False)
    places = jnp.arange(number_of)

    def named(tallies, offset_by):
        used = int((tallies > 0).sum())
        fixed = max(1, used // 4)
        passed = fixed + (places - fixed + offset_by * (used - fixed)) % max(1, number_of - fixed)
        return jnp.zeros((number_of,), jnp.int32).at[order[jnp.where(places < fixed, places, passed)]].set(jnp.asarray(tallies, jnp.int32))

    tallies = jnp.where(number % 4 == 0, named(packed, number // 4), named(ordinary, number - number // 4 - 1))
    mixed = jax.random.permutation(jax.random.fold_in(own, 3), number_of)
    source_of, sink = mixed[0:number_of // 2 * 2:2], mixed[1:number_of // 2 * 2:2]
    margin = jnp.minimum(tallies[source_of] - 1, bound - tallies[sink]) // 2
    margin = jnp.where((source_of == order[0]) | (sink == order[0]) | (tallies[sink] == 0), 0, jnp.maximum(margin, 0))
    passed = jax.random.randint(jax.random.fold_in(own, 4), (number_of // 2,), 0, 1 << 20) % (margin + 1)
    tallies = tallies.at[source_of].add(-passed).at[sink].add(passed)
    labels = jnp.searchsorted(jnp.cumsum(tallies), jnp.arange(rows * top), side="right").astype(jnp.int32)
    grid = labels.reshape(top, rows).T
    grid = grid[jax.random.permutation(jax.random.fold_in(own, 1), rows)]
    offset_by = jax.random.randint(jax.random.fold_in(own, 2), (rows, 1), 0, top)
    return jnp.take_along_axis(grid, (jnp.arange(top)[None, :] + offset_by) % top, axis=1)


def shares(count, total, bound, lean, full):
    loads = [(1 << 20) // math.isqrt(rank ** lean) + 1 for rank in range(1, count + 1)]
    largest = bound if full else min(bound, max(-(-total // count), total * loads[0] // sum(loads)))
    least = 1 if total - largest >= count - 1 else 0
    counts, spare = [largest] + [least] * (count - 1), total - largest - least * (count - 1)
    while spare > 0:
        free = [i for i in range(1, count) if counts[i] < largest] or [i for i in range(1, count) if counts[i] < bound]
        whole, budget = sum([loads[i] for i in free]), spare
        for i in free:
            addition = min(bound - counts[i], max(1, budget * loads[i] // whole), spare)
            counts[i] = counts[i] + addition
            spare = spare - addition
    return np.array(counts)


def scatter_about(key, dims, scale, bound, cuts=(), kind=jnp.bfloat16):
    drawn = scale * jax.random.normal(key, dims, jnp.float32)
    if cuts:
        drawn = drawn * block_levels(key, dims, cuts, -0.22, 0.18)
    return jnp.clip(drawn, -bound, bound).astype(kind)


def setup_inputs(seed: int = 0, part: int = 0) -> dict:
    keys = jax.random.split(jax.random.key(seed), 10)
    part_splits = jax.random.split(jax.random.fold_in(keys[9], part), 10)
    attn_heads = scatter_about(part_splits[0], (TOKENS, ATT), 1.0, 6.0, ((0, 16),))
    residual = scatter_about(part_splits[1], (TOKENS, D), 1.0, 6.0, ((0, 16),))
    w_out = scatter_about(keys[2], (ATT, D), ATT ** -0.5, 0.09375, ((0, 16),))
    norm_gain = jnp.clip(1.0 + 0.18 * jax.random.normal(keys[3], (D,), jnp.float32), 0.1, 1.9)
    expert_ids_keys = jax.random.split(jax.random.fold_in(part_splits[4], 1), TOKENS // TOK_DEV)
    expert_ids_turns = jax.random.permutation(jax.random.fold_in(part_splits[4], 3), TOKENS // TOK_DEV)
    expert_ids = jax.vmap(lambda own, number: routed_block(jax.random.fold_in(part_splits[4], 2), own, number, TOK_DEV, EXPERTS, TOPK, CAP, 2))(expert_ids_keys, expert_ids_turns).reshape((TOKENS, TOPK))
    route_num = plant(jax.random.randint(part_splits[5], (TOKENS, TOPK), 1, 17), jax.random.fold_in(part_splits[5], 1), 1, 16).astype(jnp.int32)
    w_gate = scatter_about(keys[6], (EXPERTS, D, FFE), D ** -0.5, 0.125, ((0, 16),))
    w_up = scatter_about(keys[7], (EXPERTS, D, FFE), D ** -0.5, 0.125, ((0, 16),))
    w_down = scatter_about(keys[8], (EXPERTS, FFE, D), FFE ** -0.5, 0.21875, ((0, 16),))
    return dict(attn_heads=attn_heads, residual=residual, w_out=w_out, norm_gain=norm_gain, expert_ids=expert_ids, route_num=route_num, w_gate=w_gate, w_up=w_up, w_down=w_down)


epsilon = 1e-06

def rms_scale(tensor, norm_gain):
    values = tensor.astype(jnp.float32)
    mean_sq = lax.optimization_barrier(jnp.mean(values * values, axis=-1, keepdims=True))
    return (values * lax.rsqrt(mean_sq + epsilon) * norm_gain).astype(jnp.bfloat16)

def reference(attn_heads, residual, w_out, norm_gain, expert_ids, route_num, w_gate, w_up, w_down):
    projected = jnp.dot(attn_heads, w_out, preferred_element_type=jnp.float32)
    mid_state = (residual.astype(jnp.float32) + projected).astype(jnp.bfloat16)
    normed = rms_scale(mid_state, norm_gain)
    numer = route_num.astype(jnp.float32)
    weights = numer / lax.optimization_barrier(jnp.sum(numer, axis=1, keepdims=True))
    ids_dev = expert_ids.reshape(N_EXPERT, TOK_DEV * TOPK)
    onehot = (ids_dev[:, :, None] == jnp.arange(EXPERTS, dtype=jnp.int32)[None, None, :]).astype(jnp.int32)
    before = jnp.cumsum(onehot, axis=1) - onehot
    slot_index = lax.optimization_barrier(jnp.sum(before * onehot, axis=2))
    device_of = jnp.arange(N_EXPERT, dtype=jnp.int32)[:, None]
    row_index = (device_of * CAP + slot_index).reshape(-1).astype(jnp.int32)
    flat_ids = expert_ids.reshape(-1)
    token_index = jnp.arange(TOKENS * TOPK, dtype=jnp.int32) // TOPK
    token_of_row = jnp.full((EXPERTS, N_EXPERT * CAP), TOKENS, jnp.int32).at[flat_ids, row_index].set(token_index)
    weight_of_row = jnp.zeros((EXPERTS, N_EXPERT * CAP), jnp.float32).at[flat_ids, row_index].set(weights.reshape(-1))
    padded = jnp.concatenate([normed, jnp.zeros((1, D), jnp.bfloat16)], axis=0)

    def one_expert(running, inputs):
        gate_mat, up_mat, down_mat, token_rows, row_weights = inputs
        row_block = padded[token_rows]
        gate_act = jnp.dot(row_block, gate_mat, preferred_element_type=jnp.float32)
        up_act = jnp.dot(row_block, up_mat, preferred_element_type=jnp.float32)
        hidden = (jax.nn.silu(gate_act) * up_act).astype(jnp.bfloat16)
        result = jnp.dot(hidden, down_mat, preferred_element_type=jnp.float32).astype(jnp.bfloat16)
        running = running.at[token_rows].add(row_weights[:, None] * result.astype(jnp.float32))
        return (running, None)
    start = jnp.zeros((TOKENS + 1, D), jnp.float32)
    running, _ = lax.scan(one_expert, start, (w_gate, w_up, w_down, token_of_row, weight_of_row))
    expert_out = running[:TOKENS].astype(jnp.bfloat16)
    return (mid_state, expert_out)
```

```python
import functools

import jax
import jax.numpy as jnp
from jax import lax
from jax.experimental import pallas as pl
from jax.experimental.pallas import tpu as pltpu
from jax.sharding import PartitionSpec as P

epsilon = 1e-06
MESH = pl.DeviceIdType.MESH
F32, BF16 = jnp.float32, jnp.bfloat16
VMEM_BYTES = 56 * 1024 * 1024
DMA, VM = pltpu.SemaphoreType.DMA, pltpu.VMEM


def rms_scale(tensor, norm_gain):
    values = tensor.astype(F32)
    mean_sq = jnp.mean(values * values, axis=-1, keepdims=True)
    return (values * lax.rsqrt(mean_sq + epsilon) * norm_gain).astype(BF16)


def tile(size, most):
    return next(t for t in range(min(size, most), 0, -1) if size % t == 0 and (t % 128 == 0 or t == size))


class Place:
    def __init__(self, depth):
        e = lax.axis_index("expert")
        self.depth = depth
        self.z, self.x, self.c = e // 4, (e // 2) % 2, e % 2

    def back(self, k):
        return lax.rem(self.z + self.depth - k, self.depth)

    def at(self, z=None, x=None, c=None):
        z = self.z if z is None else z
        x = self.x if x is None else x
        c = self.c if c is None else c
        return {"expert": (z * 2 + x) * 2 + c}

    def others(self):
        targets = [self.at(z=lax.rem(self.z + k, self.depth)) for k in range(1, self.depth)]
        return targets + [self.at(x=1 - self.x), self.at(c=1 - self.c)]


def greet(targets):
    barrier = pltpu.get_barrier_semaphore()
    for target in targets:
        pl.semaphore_signal(barrier, inc=1, device_id=target, device_id_type=MESH)
    pl.semaphore_wait(barrier, len(targets))


def push(src, dst, sems, i, target):
    copy = pltpu.make_async_remote_copy(
        src_ref=src, dst_ref=dst, send_sem=sems[0].at[i], recv_sem=sems[1].at[i], device_id=target, device_id_type=MESH
    )
    copy.start()
    return copy


class Gather:
    def __init__(self, place, slot, zs, xs, cs):
        self.p, self.slot, self.zs, self.xs, self.cs = place, slot, zs, xs, cs
        self.sent = []

    def start(self):
        p = self.p
        own = self.slot(p.z, p.x, p.c)
        self.landed = {}
        for k in range(1, p.depth):
            self.sent.append(push(own, own, self.zs, k, p.at(z=lax.rem(p.z + k, p.depth))))
        self.x_on(0)
        self.c_on(0, p.z, p.x)

    def x_on(self, k):
        p = self.p
        ref = self.slot(p.back(k), p.x, p.c)
        self.sent.append(push(ref, ref, self.xs, k, p.at(x=1 - p.x)))

    def c_on(self, i, z, x):
        ref = self.slot(z, x, self.p.c)
        self.sent.append(push(ref, ref, self.cs, i, self.p.at(c=1 - self.p.c)))

    def wait(self, ref, sems, i):
        pltpu.make_async_remote_copy(
            src_ref=ref, dst_ref=ref, send_sem=sems[0].at[i], recv_sem=sems[1].at[i],
            device_id=self.p.at(c=1 - self.p.c), device_id_type=MESH,
        ).wait_recv()

    def from_z(self, k):
        p = self.p
        if k:
            self.wait(self.slot(p.back(k), p.x, p.c), self.zs, k)
            self.x_on(k)
            self.c_on(k, p.back(k), p.x)

    def from_x(self, k):
        p = self.p
        self.wait(self.slot(p.back(k), 1 - p.x, p.c), self.xs, k)
        self.c_on(p.depth + k, p.back(k), 1 - p.x)

    def near(self, k):
        p = self.p
        self.wait(self.slot(p.back(k), p.x, 1 - p.c), self.cs, k)

    def far(self, k):
        p = self.p
        self.wait(self.slot(p.back(k), 1 - p.x, 1 - p.c), self.cs, p.depth + k)

    def finish(self):
        for copy in self.sent:
            copy.wait_send()


def project_kernel(depth, attn, resid, w, gain, mid, normed, wbuf, act, rbuf, moving, landed, acc, *sems):
    ys, zs, xs, cs = [(sems[2 * i], sems[2 * i + 1]) for i in range(4)]
    p = Place(depth)
    g = lax.axis_index("groups")
    partner = {"groups": 1 - g}
    toks, feats = resid.shape
    rows, half = w.shape[0], feats // 2
    mine = pl.ds(pl.multiple_of(g * half, half), half)
    theirs = pl.ds(pl.multiple_of((1 - g) * half, half), half)

    def slot(z, x, c):
        return wbuf.at[z * 2 + x, pl.ds(pl.multiple_of(c * rows, rows), rows), :]

    greet(p.others() + [partner])
    wbuf[p.z * 2 + p.x, pl.ds(pl.multiple_of(p.c * rows, rows), rows), :] = w[:, mine]
    gather = Gather(p, slot, zs, xs, cs)
    gather.start()
    give = [
        push(attn, act.at[pl.ds(toks, toks), :], ys, 0, partner),
        push(resid.at[:, theirs], rbuf, ys, 1, partner),
    ]
    act[pl.ds(0, toks), :] = attn[...]
    acc[...] = jnp.zeros_like(acc)
    wide = tile(half, 256)

    def add(block):
        left = act[:, pl.ds(pl.multiple_of(block * 2 * rows, 2 * rows), 2 * rows)]

        def step(j, _):
            cols = pl.ds(pl.multiple_of(j * wide, wide), wide)
            acc[:, cols] += jnp.dot(left, wbuf[block, :, cols], preferred_element_type=F32)
            return 0

        lax.fori_loop(0, half // wide, step, 0)

    def both(k):
        if k == 0:
            for copy in give:
                copy.wait_recv()
        gather.near(k)
        add(p.back(k) * 2 + p.x)
        gather.far(k)
        add(p.back(k) * 2 + 1 - p.x)

    for k in range(depth):
        gather.from_z(k)
        gather.from_x(k)
        if k >= 2:
            both(k - 2)
    for k in range(max(depth - 2, 0), depth):
        both(k)

    moving[...] = (rbuf[...].astype(F32) + acc[pl.ds(toks, toks), :]).astype(BF16)
    back = push(moving, landed, ys, 2, partner)
    mid[:, mine] = (resid[:, mine].astype(F32) + acc[pl.ds(0, toks), :]).astype(BF16)
    back.wait_recv()
    mid[:, theirs] = landed[...]
    values = mid[...].astype(F32)
    mean_sq = jnp.sum(values * values, axis=-1, keepdims=True) * (1.0 / feats)
    normed[...] = (values * lax.rsqrt(mean_sq + epsilon) * gain[...]).astype(BF16)
    for copy in give + [back]:
        copy.wait_send()
    gather.finish()


def project(attn_heads, residual, w_out, gain, n):
    toks, feats = residual.shape
    rows, half = w_out.shape[0], feats // 2
    depth = n // 4
    vmem = pl.BlockSpec(memory_space=pltpu.VMEM)
    out = jax.ShapeDtypeStruct((toks, feats), BF16)
    counts = [3, 3, depth, depth, depth, depth, 2 * depth, 2 * depth]
    return pl.pallas_call(
        functools.partial(project_kernel, depth),
        out_shape=(out, out),
        in_specs=[vmem] * 4,
        out_specs=(vmem, vmem),
        scratch_shapes=[
            VM((2 * depth, 2 * rows, half), BF16),
            VM((2 * toks, attn_heads.shape[1]), BF16),
            VM((toks, half), BF16),
            VM((toks, half), BF16),
            VM((toks, half), BF16),
            VM((2 * toks, half), F32),
        ]
        + [DMA((count,)) for count in counts],
        compiler_params=pltpu.CompilerParams(collective_id=0, has_side_effects=True, vmem_limit_bytes=VMEM_BYTES),
        name="project",
    )(attn_heads, residual, w_out, gain)


def expert_kernel(
    depth, normed, share, wg_hbm, wu_hbm, wd_hbm, out,
    tok, part, cland, xland, zland, hidden, wg, wu, wd, load, *sems,
):
    zs, xs, cs, rz, rx, rc = [(sems[2 * i], sems[2 * i + 1]) for i in range(6)]
    p = Place(depth)
    toks, feats = normed.shape
    hid = wg.shape[1]
    mine = pl.ds(pl.multiple_of(p.c * toks, toks), toks)
    theirs = pl.ds(pl.multiple_of((1 - p.c) * toks, toks), toks)

    loads = [pltpu.make_async_copy(s, d, load.at[i]) for i, (s, d) in enumerate([(wg_hbm, wg), (wu_hbm, wu), (wd_hbm, wd)])]
    for copy in loads:
        copy.start()

    def slot(z, x, c):
        return tok.at[z * 2 + x, pl.ds(pl.multiple_of(c * toks, toks), toks), :]

    greet(p.others())
    tok[p.z * 2 + p.x, mine, :] = normed[...]
    gather = Gather(p, slot, zs, xs, cs)
    gather.start()
    sent = gather.sent
    wide_h, wide_d = tile(hid, 256), tile(feats, 256)

    def compute(block):
        def up(j, _):
            cols = pl.ds(pl.multiple_of(j * wide_h, wide_h), wide_h)
            gate = jnp.dot(tok[block], wg[:, cols], preferred_element_type=F32)
            lift = jnp.dot(tok[block], wu[:, cols], preferred_element_type=F32)
            hidden[:, cols] = (gate / (1.0 + jnp.exp(-gate)) * lift).astype(BF16)
            return 0

        def down(j, _):
            cols = pl.ds(pl.multiple_of(j * wide_d, wide_d), wide_d)
            y = jnp.dot(hidden[...], wd[:, cols], preferred_element_type=F32).astype(BF16)
            part[block, :, cols] = (y.astype(F32) * share[block]).astype(BF16)
            return 0

        lax.fori_loop(0, hid // wide_h, up, 0)
        lax.fori_loop(0, feats // wide_d, down, 0)

    core, across, along = {}, {}, {}

    def blocks(k):
        return p.back(k) * 2 + 1 - p.x, p.back(k) * 2 + p.x

    def first(k):
        far, near = blocks(k)
        gather.from_z(k)
        gather.from_x(k)
        if k == 0:
            for copy in loads:
                copy.wait()
        for i, block in ((depth + k, far), (k, near)):
            (gather.near if i < depth else gather.far)(k)
            compute(block)
            core[i] = push(part.at[block, theirs, :], cland.at[block], rc, i, p.at(c=1 - p.c))

    def add_to(block, ref):
        part[block, mine, :] = (part[block, mine, :].astype(F32) + ref.astype(F32)).astype(BF16)

    def second(k):
        far, near = blocks(k)
        core[depth + k].wait_recv()
        add_to(far, cland[far])
        across[k] = push(part.at[far, mine, :], xland.at[k], rx, k, p.at(x=1 - p.x))
        core[k].wait_recv()
        add_to(near, cland[near])

    def third(k):
        _, near = blocks(k)
        across[k].wait_recv()
        if k:
            add_to(near, xland[k])
            along[k] = push(part.at[near, mine, :], zland.at[k - 1], rz, k - 1, p.at(z=p.back(k)))

    for t in range(depth + 2):
        if t < depth:
            first(t)
        if 0 <= t - 1 < depth:
            second(t - 1)
        if 0 <= t - 2 < depth:
            third(t - 2)

    total = part[p.z * 2 + p.x, mine, :].astype(F32) + xland[0].astype(F32)
    for k in range(1, depth):
        along[k].wait_recv()
        total = total + zland[k - 1].astype(F32)
    out[...] = total.astype(BF16)
    for copy in list(core.values()) + list(across.values()) + list(along.values()):
        copy.wait_send()
    gather.finish()


def experts(normed, share, w_gate, w_up, w_down, n):
    toks, feats = normed.shape
    hid = w_gate.shape[1]
    depth = n // 4
    vmem = pl.BlockSpec(memory_space=pltpu.VMEM)
    hbm = pl.BlockSpec(memory_space=pl.ANY)
    lots = max(depth - 1, 1)
    counts = [depth, depth, depth, depth, 2 * depth, 2 * depth, lots, lots, depth, depth, 2 * depth, 2 * depth]
    return pl.pallas_call(
        functools.partial(expert_kernel, depth),
        out_shape=jax.ShapeDtypeStruct((toks, feats), BF16),
        in_specs=[vmem, vmem, hbm, hbm, hbm],
        out_specs=vmem,
        scratch_shapes=[
            VM((2 * depth, 2 * toks, feats), BF16),
            VM((2 * depth, 2 * toks, feats), BF16),
            VM((2 * depth, toks, feats), BF16),
            VM((depth, toks, feats), BF16),
            VM((lots, toks, feats), BF16),
            VM((2 * toks, hid), BF16),
            VM(w_gate.shape, BF16),
            VM(w_up.shape, BF16),
            VM(w_down.shape, BF16),
            DMA((3,)),
        ]
        + [DMA((count,)) for count in counts],
        compiler_params=pltpu.CompilerParams(collective_id=1, has_side_effects=True, vmem_limit_bytes=VMEM_BYTES),
        name="experts",
    )(normed, share, w_gate, w_up, w_down)


def dense(attn_heads, residual, w_out, norm_gain, expert_ids, route_num, w_gate, w_up, w_down):
    n = lax.axis_size("expert")
    toks = residual.shape[0]
    numer = route_num.astype(F32)
    weights = numer / jnp.sum(numer, axis=1, keepdims=True)
    chosen = expert_ids[:, :, None] == jnp.arange(n, dtype=jnp.int32)[None, None, :]
    table = jnp.sum(jnp.where(chosen, weights[:, :, None], 0.0), axis=1)
    tables = lax.all_gather(table.T, "expert", axis=0)
    share = lax.dynamic_index_in_dim(tables, lax.axis_index("expert"), axis=1, keepdims=False)
    share = share.reshape(n // 2, 2 * toks, 1)
    mid_state, normed = project(attn_heads, residual, w_out, norm_gain[None, :], n)
    return mid_state, experts(normed, share, w_gate[0], w_up[0], w_down[0], n)


def sparse(attn_heads, residual, w_out, norm_gain, expert_ids, route_num, w_gate, w_up, w_down):
    tok_rows = attn_heads.shape[0]
    feature_count = residual.shape[1]
    gathered = lax.all_gather(w_out, "expert", axis=0, tiled=True)
    projected = jnp.dot(attn_heads, gathered, preferred_element_type=F32)
    mid_state = (residual.astype(F32) + projected).astype(BF16)
    n_experts = lax.axis_size("expert")
    top_count = expert_ids.shape[1]
    capacity = tok_rows * top_count * 5 // (4 * n_experts)
    onehot = expert_ids[:, :, None] == jnp.arange(n_experts, dtype=jnp.int32)[None, None, :]
    order = jnp.arange(tok_rows, dtype=jnp.int32)
    earlier = (order[:, None] > order[None, :]).astype(BF16)
    before = jnp.dot(earlier, jnp.any(onehot, axis=1).astype(BF16), preferred_element_type=F32)
    slot_index = jnp.sum(jnp.where(onehot, before[:, None, :], 0.0), axis=2).astype(jnp.int32)
    position = expert_ids * capacity + slot_index
    payload = rms_scale(mid_state, norm_gain)
    spots = jnp.arange(n_experts * capacity, dtype=jnp.int32)
    pick = jnp.any(position[None] == spots[:, None, None], axis=2).astype(BF16)
    sendbuf = jnp.dot(pick, payload, preferred_element_type=F32).astype(BF16)
    sendbuf = sendbuf.reshape(n_experts, capacity, feature_count)
    received = lax.all_to_all(sendbuf, "expert", split_axis=0, concat_axis=0, tiled=True)
    sources, slot_count, _ = received.shape
    row_block = received.reshape(sources * slot_count, feature_count)
    gate_act = jnp.dot(row_block, w_gate[0], preferred_element_type=F32)
    up_act = jnp.dot(row_block, w_up[0], preferred_element_type=F32)
    hidden = (jax.nn.silu(gate_act) * up_act).astype(BF16)
    result = jnp.dot(hidden, w_down[0], preferred_element_type=F32).astype(BF16)
    result = result.reshape(sources, slot_count, feature_count)
    returned = lax.all_to_all(result, "expert", split_axis=0, concat_axis=0, tiled=True)
    returned = returned.reshape(n_experts * capacity, feature_count)
    numer = route_num.astype(F32)
    weights = numer / jnp.sum(numer, axis=1, keepdims=True)
    hit = position[:, :, None] == spots[None, None, :]
    blend = jnp.sum(jnp.where(hit, weights[:, :, None], 0.0), axis=1)
    expert_out = jnp.dot(blend, returned.astype(F32), precision=lax.Precision.HIGHEST).astype(BF16)
    return (mid_state, expert_out)


def solution(mesh):
    n, groups = mesh.shape["expert"], mesh.shape["groups"]
    in_specs = (
        P(("groups", "expert"), None),
        P(("groups", "expert"), None),
        P("expert", None),
        P(),
        P(("groups", "expert"), None),
        P(("groups", "expert"), None),
        P("expert", None, None),
        P("expert", None, None),
        P("expert", None, None),
    )
    out_specs = (P(("groups", "expert"), None), P(("groups", "expert"), None))

    def per_device(*args):
        residual, w_out, ids, w_gate = args[1], args[2], args[4], args[6]
        toks, feats = residual.shape
        held = 2 * feats * (toks * (3 * n + n // 2) + 3 * w_gate.shape[2])
        few = n <= 2 * ids.shape[1] and held <= VMEM_BYTES * 3 // 4
        even = n % 4 == 0 and groups == 2 and feats % 256 == 0 and w_out.shape[0] % 64 == 0 and toks % 16 == 0
        return (dense if few and even else sparse)(*args)

    return jax.shard_map(per_device, mesh=mesh, in_specs=in_specs, out_specs=out_specs, check_vma=False)
```

```python
import functools

import jax
import jax.numpy as jnp
from jax import lax
from jax.experimental import pallas as pl
from jax.experimental.pallas import tpu as pltpu
from jax.sharding import PartitionSpec as P

epsilon = 1e-06
MESH = pl.DeviceIdType.MESH
F32, BF16 = jnp.float32, jnp.bfloat16
VMEM_BYTES = 56 * 1024 * 1024
DMA, VM = pltpu.SemaphoreType.DMA, pltpu.VMEM


def rms_scale(tensor, norm_gain):
    values = tensor.astype(F32)
    mean_sq = jnp.mean(values * values, axis=-1, keepdims=True)
    return (values * lax.rsqrt(mean_sq + epsilon) * norm_gain).astype(BF16)


def tile(size, most):
    return next(t for t in range(min(size, most), 0, -1) if size % t == 0 and (t % 128 == 0 or t == size))


class Place:
    def __init__(self, depth):
        e = lax.axis_index("expert")
        self.depth = depth
        self.z, self.x, self.c = e // 4, (e // 2) % 2, e % 2

    def source(self, k):
        if k == 0:
            return self.z
        above = self.depth - 1 - self.z
        near = jnp.minimum(self.z, above)
        level = self.z - (k + 1) // 2 if k % 2 else self.z + k // 2
        beyond = jnp.where(self.z < above, self.z + k - near, self.z - k + near)
        return jnp.where(k <= 2 * near, level, beyond)

    def at(self, z=None, x=None, c=None):
        z = self.z if z is None else z
        x = self.x if x is None else x
        c = self.c if c is None else c
        return {"expert": (z * 2 + x) * 2 + c}

    def others(self):
        targets = [self.at(z=lax.rem(self.z + k, self.depth)) for k in range(1, self.depth)]
        return targets + [self.at(x=1 - self.x), self.at(c=1 - self.c)]


def greet(targets):
    barrier = pltpu.get_barrier_semaphore()
    for target in targets:
        pl.semaphore_signal(barrier, inc=1, device_id=target, device_id_type=MESH)
    pl.semaphore_wait(barrier, len(targets))


def push(src, dst, sems, i, target):
    copy = pltpu.make_async_remote_copy(
        src_ref=src, dst_ref=dst, send_sem=sems[0].at[i], recv_sem=sems[1].at[i], device_id=target, device_id_type=MESH
    )
    copy.start()
    return copy


class Gather:
    def __init__(self, place, slot, up, down, across, core):
        self.p, self.slot, self.up, self.down, self.across, self.core = place, slot, up, down, across, core
        self.sources = [place.source(k) for k in range(place.depth)]

    def copy(self, z, x, c, sems, i, target):
        ref = self.slot(z, x, c)
        return pltpu.make_async_remote_copy(
            src_ref=ref, dst_ref=ref, send_sem=sems[0].at[i], recv_sem=sems[1].at[i],
            device_id=target, device_id_type=MESH,
        )

    def hops(self, z):
        p = self.p
        up = self.copy(z, p.x, p.c, self.up, z, p.at(z=jnp.minimum(p.z + 1, p.depth - 1)))
        down = self.copy(z, p.x, p.c, self.down, z, p.at(z=jnp.maximum(p.z - 1, 0)))
        return ((z <= p.z) & (p.z < p.depth - 1), up), ((z >= p.z) & (p.z > 0), down)

    def others(self, z):
        p = self.p
        over = self.copy(z, p.x, p.c, self.across, z, p.at(x=1 - p.x))
        near = self.copy(z, p.x, p.c, self.core, z, p.at(c=1 - p.c))
        far = self.copy(z, 1 - p.x, p.c, self.core, p.depth + z, p.at(c=1 - p.c))
        return over, near, far

    def from_z(self, k):
        p, z = self.p, self.sources[k]
        if k:
            up, down = [copy for _, copy in self.hops(z)]
            pl.when(z < p.z)(up.wait_recv)
            pl.when(z > p.z)(down.wait_recv)
        for made, copy in self.hops(z):
            pl.when(made)(copy.start)
        over, near, _ = self.others(z)
        over.start()
        near.start()

    def from_x(self, k):
        p, z = self.p, self.sources[k]
        self.copy(z, 1 - p.x, p.c, self.across, z, p.at(x=1 - p.x)).wait_recv()
        self.others(z)[2].start()

    def near(self, k):
        p, z = self.p, self.sources[k]
        self.copy(z, p.x, 1 - p.c, self.core, z, p.at(c=1 - p.c)).wait_recv()

    def far(self, k):
        p, z = self.p, self.sources[k]
        self.copy(z, 1 - p.x, 1 - p.c, self.core, p.depth + z, p.at(c=1 - p.c)).wait_recv()

    def finish(self):
        for z in self.sources:
            for made, copy in self.hops(z):
                pl.when(made)(copy.wait_send)
            for copy in self.others(z):
                copy.wait_send()


def project_kernel(
    depth, attn, resid, w, gain, table, mid, normed, share, wbuf, act, rbuf, moving, landed, acc, tables, *sems
):
    ys, us, ds, xs, cs, tu, td, tx, tc = [(sems[2 * i], sems[2 * i + 1]) for i in range(9)]
    p = Place(depth)
    g = lax.axis_index("groups")
    partner = {"groups": 1 - g}
    toks, feats = resid.shape
    rows, half = w.shape[0], feats // 2
    mine = pl.ds(pl.multiple_of(g * half, half), half)
    theirs = pl.ds(pl.multiple_of((1 - g) * half, half), half)

    def slot(z, x, c):
        return wbuf.at[z * 2 + x, pl.ds(pl.multiple_of(c * rows, rows), rows), :]

    greet(p.others() + [partner])
    wbuf[p.z * 2 + p.x, pl.ds(pl.multiple_of(p.c * rows, rows), rows), :] = w[:, mine]
    tables[(p.z * 2 + p.x) * 2 + p.c] = table[...]
    routes = Gather(p, lambda z, x, c: tables.at[(z * 2 + x) * 2 + c], tu, td, tx, tc)
    routes.from_z(0)
    gather = Gather(p, slot, us, ds, xs, cs)
    gather.from_z(0)
    give = [
        push(attn, act.at[pl.ds(toks, toks), :], ys, 0, partner),
        push(resid.at[:, theirs], rbuf, ys, 1, partner),
    ]
    act[pl.ds(0, toks), :] = attn[...]
    acc[...] = jnp.zeros_like(acc)
    wide = tile(half, 256)

    def add(block):
        left = act[:, pl.ds(pl.multiple_of(block * 2 * rows, 2 * rows), 2 * rows)]

        def step(j, _):
            cols = pl.ds(pl.multiple_of(j * wide, wide), wide)
            acc[:, cols] += jnp.dot(left, wbuf[block, :, cols], preferred_element_type=F32)
            return 0

        lax.fori_loop(0, half // wide, step, 0)

    def both(k):
        if k == 0:
            for copy in give:
                copy.wait_recv()
        gather.near(k)
        add(gather.sources[k] * 2 + p.x)
        gather.far(k)
        add(gather.sources[k] * 2 + 1 - p.x)

    for k in range(1, depth + 1):
        if k < depth:
            routes.from_z(k)
            gather.from_z(k)
        routes.from_x(k - 1)
        gather.from_x(k - 1)
        if k >= 3:
            both(k - 3)
    for k in range(max(depth - 2, 0), depth):
        both(k)

    moving[...] = (rbuf[...].astype(F32) + acc[pl.ds(toks, toks), :]).astype(BF16)
    back = push(moving, landed, ys, 2, partner)
    for k in range(depth):
        routes.near(k)
        routes.far(k)
    share[...] = tables[:, lax.axis_index("expert"), :]
    mid[:, mine] = (resid[:, mine].astype(F32) + acc[pl.ds(0, toks), :]).astype(BF16)
    back.wait_recv()
    mid[:, theirs] = landed[...]
    values = mid[...].astype(F32)
    mean_sq = jnp.sum(values * values, axis=-1, keepdims=True) * (1.0 / feats)
    normed[...] = (values * lax.rsqrt(mean_sq + epsilon) * gain[...]).astype(BF16)
    for copy in give + [back]:
        copy.wait_send()
    gather.finish()
    routes.finish()


def project(attn_heads, residual, w_out, gain, table, n):
    toks, feats = residual.shape
    rows, half = w_out.shape[0], feats // 2
    depth = n // 4
    vmem = pl.BlockSpec(memory_space=pltpu.VMEM)
    out = jax.ShapeDtypeStruct((toks, feats), BF16)
    counts = [3, 3] + 2 * (6 * [depth] + 2 * [2 * depth])
    return pl.pallas_call(
        functools.partial(project_kernel, depth),
        out_shape=(out, out, jax.ShapeDtypeStruct((n, toks), F32)),
        in_specs=[vmem] * 5,
        out_specs=(vmem, vmem, vmem),
        scratch_shapes=[
            VM((2 * depth, 2 * rows, half), BF16),
            VM((2 * toks, attn_heads.shape[1]), BF16),
            VM((toks, half), BF16),
            VM((toks, half), BF16),
            VM((toks, half), BF16),
            VM((2 * toks, half), F32),
            VM((n,) + table.shape, F32),
        ]
        + [DMA((count,)) for count in counts],
        compiler_params=pltpu.CompilerParams(collective_id=0, has_side_effects=True, vmem_limit_bytes=VMEM_BYTES),
        name="project",
    )(attn_heads, residual, w_out, gain, table)


def expert_kernel(
    depth, normed, share, wg_hbm, wu_hbm, wd_hbm, out,
    tok, part, cland, xland, zland, hidden, wg, wu, wd, load, *sems,
):
    us, ds, xs, cs, rz, rx, rc = [(sems[2 * i], sems[2 * i + 1]) for i in range(7)]
    p = Place(depth)
    toks, feats = normed.shape
    hid = wg.shape[1]
    mine = pl.ds(pl.multiple_of(p.c * toks, toks), toks)
    theirs = pl.ds(pl.multiple_of((1 - p.c) * toks, toks), toks)

    loads = [pltpu.make_async_copy(s, d, load.at[i]) for i, (s, d) in enumerate([(wg_hbm, wg), (wu_hbm, wu), (wd_hbm, wd)])]
    for copy in loads:
        copy.start()

    def slot(z, x, c):
        return tok.at[z * 2 + x, pl.ds(pl.multiple_of(c * toks, toks), toks), :]

    greet(p.others())
    tok[p.z * 2 + p.x, mine, :] = normed[...]
    gather = Gather(p, slot, us, ds, xs, cs)
    gather.from_z(0)
    wide_h, wide_d = tile(hid, 256), tile(feats, 256)

    def compute(block):
        def up(j, _):
            cols = pl.ds(pl.multiple_of(j * wide_h, wide_h), wide_h)
            gate = jnp.dot(tok[block], wg[:, cols], preferred_element_type=F32)
            lift = jnp.dot(tok[block], wu[:, cols], preferred_element_type=F32)
            hidden[:, cols] = (gate / (1.0 + jnp.exp(-gate)) * lift).astype(BF16)
            return 0

        def down(j, _):
            cols = pl.ds(pl.multiple_of(j * wide_d, wide_d), wide_d)
            y = jnp.dot(hidden[...], wd[:, cols], preferred_element_type=F32).astype(BF16)
            part[block, :, cols] = (y.astype(F32) * share[block]).astype(BF16)
            return 0

        lax.fori_loop(0, hid // wide_h, up, 0)
        lax.fori_loop(0, feats // wide_d, down, 0)

    core, across = {}, {}

    def blocks(k):
        z = gather.sources[k]
        return z * 2 + 1 - p.x, z * 2 + p.x

    def first(k):
        far, near = blocks(k)
        if k + 1 < depth:
            gather.from_z(k + 1)
        gather.from_x(k)
        if k == 0:
            for copy in loads:
                copy.wait()
        for name, block in (("far", far), ("near", near)):
            (gather.far if name == "far" else gather.near)(k)
            compute(block)
            core[name, k] = push(part.at[block, theirs, :], cland.at[block], rc, block, p.at(c=1 - p.c))

    def add_to(block, ref):
        part[block, mine, :] = (part[block, mine, :].astype(F32) + ref.astype(F32)).astype(BF16)

    def second(k):
        far, near = blocks(k)
        core["far", k].wait_recv()
        add_to(far, cland[far])
        z = gather.sources[k]
        across[k] = push(part.at[far, mine, :], xland.at[z], rx, z, p.at(x=1 - p.x))
        core["near", k].wait_recv()
        add_to(near, cland[near])

    def along_to(k):
        dest = lax.rem(p.z + k, depth)
        return pltpu.make_async_remote_copy(
            src_ref=part.at[dest * 2 + p.x, mine, :], dst_ref=zland.at[k - 1], send_sem=rz[0].at[k - 1],
            recv_sem=rz[1].at[k - 1], device_id=p.at(z=dest), device_id_type=MESH,
        )

    def third(k):
        _, near = blocks(k)
        across[k].wait_recv()
        if k:
            z = gather.sources[k]
            add_to(near, xland[z])
            by = lax.rem(z - p.z + depth, depth)
            pltpu.make_async_remote_copy(
                src_ref=part.at[near, mine, :], dst_ref=zland.at[by - 1], send_sem=rz[0].at[by - 1],
                recv_sem=rz[1].at[by - 1], device_id=p.at(z=z), device_id_type=MESH,
            ).start()

    for t in range(depth + 2):
        if t < depth:
            first(t)
        if 0 <= t - 1 < depth:
            second(t - 1)
        if 0 <= t - 2 < depth:
            third(t - 2)

    total = part[p.z * 2 + p.x, mine, :].astype(F32) + xland[p.z].astype(F32)
    for k in range(1, depth):
        along_to(k).wait_recv()
        total = total + zland[k - 1].astype(F32)
    out[...] = total.astype(BF16)
    for copy in list(core.values()) + list(across.values()) + [along_to(k) for k in range(1, depth)]:
        copy.wait_send()
    gather.finish()


def experts(normed, share, w_gate, w_up, w_down, n):
    toks, feats = normed.shape
    hid = w_gate.shape[1]
    depth = n // 4
    vmem = pl.BlockSpec(memory_space=pltpu.VMEM)
    hbm = pl.BlockSpec(memory_space=pl.ANY)
    lots = max(depth - 1, 1)
    counts = 6 * [depth] + 2 * [2 * depth] + 2 * [lots] + 2 * [depth] + 2 * [2 * depth]
    return pl.pallas_call(
        functools.partial(expert_kernel, depth),
        out_shape=jax.ShapeDtypeStruct((toks, feats), BF16),
        in_specs=[vmem, vmem, hbm, hbm, hbm],
        out_specs=vmem,
        scratch_shapes=[
            VM((2 * depth, 2 * toks, feats), BF16),
            VM((2 * depth, 2 * toks, feats), BF16),
            VM((2 * depth, toks, feats), BF16),
            VM((depth, toks, feats), BF16),
            VM((lots, toks, feats), BF16),
            VM((2 * toks, hid), BF16),
            VM(w_gate.shape, BF16),
            VM(w_up.shape, BF16),
            VM(w_down.shape, BF16),
            DMA((3,)),
        ]
        + [DMA((count,)) for count in counts],
        compiler_params=pltpu.CompilerParams(collective_id=1, has_side_effects=True, vmem_limit_bytes=VMEM_BYTES),
        name="experts",
    )(normed, share, w_gate, w_up, w_down)


def dense(attn_heads, residual, w_out, norm_gain, expert_ids, route_num, w_gate, w_up, w_down):
    n = lax.axis_size("expert")
    toks = residual.shape[0]
    numer = route_num.astype(F32)
    weights = numer / jnp.sum(numer, axis=1, keepdims=True)
    chosen = expert_ids[:, :, None] == jnp.arange(n, dtype=jnp.int32)[None, None, :]
    table = jnp.sum(jnp.where(chosen, weights[:, :, None], 0.0), axis=1)
    mid_state, normed, share = project(attn_heads, residual, w_out, norm_gain[None, :], table.T, n)
    share = share.reshape(n // 2, 2 * toks, 1)
    return mid_state, experts(normed, share, w_gate[0], w_up[0], w_down[0], n)


def sparse(attn_heads, residual, w_out, norm_gain, expert_ids, route_num, w_gate, w_up, w_down):
    tok_rows = attn_heads.shape[0]
    feature_count = residual.shape[1]
    gathered = lax.all_gather(w_out, "expert", axis=0, tiled=True)
    projected = jnp.dot(attn_heads, gathered, preferred_element_type=F32)
    mid_state = (residual.astype(F32) + projected).astype(BF16)
    n_experts = lax.axis_size("expert")
    top_count = expert_ids.shape[1]
    capacity = tok_rows * top_count * 5 // (4 * n_experts)
    onehot = expert_ids[:, :, None] == jnp.arange(n_experts, dtype=jnp.int32)[None, None, :]
    order = jnp.arange(tok_rows, dtype=jnp.int32)
    earlier = (order[:, None] > order[None, :]).astype(BF16)
    before = jnp.dot(earlier, jnp.any(onehot, axis=1).astype(BF16), preferred_element_type=F32)
    slot_index = jnp.sum(jnp.where(onehot, before[:, None, :], 0.0), axis=2).astype(jnp.int32)
    position = expert_ids * capacity + slot_index
    payload = rms_scale(mid_state, norm_gain)
    spots = jnp.arange(n_experts * capacity, dtype=jnp.int32)
    pick = jnp.any(position[None] == spots[:, None, None], axis=2).astype(BF16)
    sendbuf = jnp.dot(pick, payload, preferred_element_type=F32).astype(BF16)
    sendbuf = sendbuf.reshape(n_experts, capacity, feature_count)
    received = lax.all_to_all(sendbuf, "expert", split_axis=0, concat_axis=0, tiled=True)
    sources, slot_count, _ = received.shape
    row_block = received.reshape(sources * slot_count, feature_count)
    gate_act = jnp.dot(row_block, w_gate[0], preferred_element_type=F32)
    up_act = jnp.dot(row_block, w_up[0], preferred_element_type=F32)
    hidden = (jax.nn.silu(gate_act) * up_act).astype(BF16)
    result = jnp.dot(hidden, w_down[0], preferred_element_type=F32).astype(BF16)
    result = result.reshape(sources, slot_count, feature_count)
    returned = lax.all_to_all(result, "expert", split_axis=0, concat_axis=0, tiled=True)
    returned = returned.reshape(n_experts * capacity, feature_count)
    numer = route_num.astype(F32)
    weights = numer / jnp.sum(numer, axis=1, keepdims=True)
    hit = position[:, :, None] == spots[None, None, :]
    blend = jnp.sum(jnp.where(hit, weights[:, :, None], 0.0), axis=1)
    expert_out = jnp.dot(blend, returned.astype(F32), precision=lax.Precision.HIGHEST).astype(BF16)
    return (mid_state, expert_out)


def solution(mesh):
    n, groups = mesh.shape["expert"], mesh.shape["groups"]
    in_specs = (
        P(("groups", "expert"), None),
        P(("groups", "expert"), None),
        P("expert", None),
        P(),
        P(("groups", "expert"), None),
        P(("groups", "expert"), None),
        P("expert", None, None),
        P("expert", None, None),
        P("expert", None, None),
    )
    out_specs = (P(("groups", "expert"), None), P(("groups", "expert"), None))

    def per_device(*args):
        residual, w_out, ids, w_gate = args[1], args[2], args[4], args[6]
        toks, feats = residual.shape
        held = 2 * feats * (toks * (3 * n + n // 2) + 3 * w_gate.shape[2])
        few = n <= 2 * ids.shape[1] and held <= VMEM_BYTES * 3 // 4
        even = n % 4 == 0 and groups == 2 and feats % 256 == 0 and w_out.shape[0] % 64 == 0 and toks % 16 == 0
        return (dense if few and even else sparse)(*args)

    return jax.shard_map(per_device, mesh=mesh, in_specs=in_specs, out_specs=out_specs, check_vma=False)
```
